512 devices in a mesh: mode: 16 (over y_hi, x), resp: 16 (over z, y_lo), dof: 2 (over core).
Axes of the slice: x: 4, y: 8 (y_hi: 4, y_lo: 2; y = y_hi * 2 + y_lo), z: 8, core: 2. Of those that a mesh axis runs over, the one named last changes fastest.
Arguments:
- modes: bfloat16 [24576, 2048], P(('mode', 'dof')), may hold values from -0.0390625 to 0.0390625
- pressure: bfloat16 [24576, 2, 4096], P(('mode', 'dof'), None, 'resp'), may hold values from -6 to 6
- tile_list: int32 [640, 2], replicated, may hold values from 0 to 63, as said below
- slab_map: int32 [1024], replicated, may hold values from 0 to 1023, as said below
Outputs:
- forces: float32 [2048, 2, 4096], P(('mode', 'dof'), None, 'resp')
The draws below stay inside these ranges and needn't reach their ends.
Inputs may be any that keep to these rules, and one draw needn't show every extreme that they name: `tile_list`: column 0 is below 16, column 1 below 64; rows may repeat. `slab_map`: blocks q * 32 to q * 32 + 31 form DOF group q; the slab blocks that a group takes come one from each DOF group, and every slab block is taken once.
All inputs are finite; a program needn't handle non-finite values.
Results may differ from the reference program's by a relative error of at most 0.0003.
Values may be sent and summed in bfloat16 or wider, within the bound.
A program may use at most 64 MiB of HBM per device.

```python
import jax
import jax.numpy as jnp
from jax import lax

M = 2048
MB = 128
RB = 64
TILES = 640
NSLAB = 32
NDOF = 24576
BROWS = 24
RESP = 4096
NMB = 16
NRB = 64


def draw_tile_list(key, part):
    mode_column = jax.random.randint(jax.random.fold_in(key, 11), (TILES,), 0, NMB)
    resp_column = jax.random.randint(jax.random.fold_in(key, 12), (TILES,), 0, NRB)
    return jnp.stack([mode_column, resp_column], axis=1).astype(jnp.int32)


def draw_slab_map(key, part):
    sender_keys = jax.random.split(jax.random.fold_in(key, 21), NSLAB)
    order_keys = jax.random.split(jax.random.fold_in(key, 22), NSLAB)
    sender_perm = jax.vmap(lambda k: jax.random.permutation(k, NSLAB))(sender_keys)
    order_perm = jax.vmap(lambda k: jax.random.permutation(k, NSLAB))(order_keys)
    group_ids = jnp.arange(NSLAB, dtype=jnp.int32)[:, None]
    local_block = sender_perm[order_perm, group_ids]
    return (order_perm * NSLAB + local_block).reshape(-1).astype(jnp.int32)


def level_of(own_key, dims, cuts, least, high):
    loudness = 1.0
    for axis_at, blocks in cuts:
        heights = jax.random.uniform(jax.random.fold_in(jax.random.fold_in(own_key, 6), axis_at), (blocks,), jnp.float32, least / len(cuts), high / len(cuts))
        loudness = loudness * jnp.repeat(jnp.exp(heights), dims[axis_at] // blocks).reshape((-1,) + (1,) * (len(dims) - 1 - axis_at))
    return loudness


def centred(key, extent, spread, limit, cuts=(), held_as=jnp.bfloat16):
    gain = level_of(key, extent, cuts, -0.22, 0.18) if cuts else 1.0
    result = jax.random.normal(key, extent, jnp.float32) * spread * gain
    return jnp.minimum(jnp.maximum(result, -limit), limit).astype(held_as)


def setup_inputs(seed: int = 0) -> dict:
    key_of = jax.random.split(jax.random.key(seed), 5)
    modes = centred(key_of[0], (NDOF, M), NDOF ** -0.5, 0.0390625, ((0, 32),))
    pressure = centred(key_of[1], (NDOF, 2, RESP), 1.0, 6.0, ((0, 32), (2, 16)))
    tile_list = draw_tile_list(jax.random.fold_in(key_of[4], 71), 0)
    slab_map = draw_slab_map(jax.random.fold_in(key_of[4], 71), 0)
    return dict(modes=modes, pressure=pressure, tile_list=tile_list, slab_map=slab_map)


def reference(modes, pressure, tile_list, slab_map):
    blocks = pressure.reshape(NDOF // BROWS, BROWS, 2 * RESP)
    aligned = jnp.take(blocks, slab_map.astype(jnp.int32), axis=0).reshape(NDOF, 2 * RESP)
    dense = jnp.dot(modes.astype(jnp.float32).T, aligned.astype(jnp.float32), precision=lax.Precision.HIGHEST, preferred_element_type=jnp.float32)
    listed = jnp.zeros((NMB, NRB), jnp.float32).at[tile_list[:, 0], tile_list[:, 1]].set(1.0)
    row_mask = jnp.repeat(listed, MB, axis=0)
    column_mask = jnp.repeat(row_mask, RB, axis=1)
    return dense.reshape(M, 2, RESP) * column_mask[:, None, :]
```

```python
import functools

import jax
import jax.numpy as jnp
from jax import lax
from jax.experimental import pallas as pl
from jax.experimental.pallas import tpu as pltpu
from jax.sharding import PartitionSpec as P

F32 = jnp.float32
BF16 = jnp.bfloat16
I16 = jnp.int16
LANES = 128
BROWS = 24
GROUP = 32
CHIPS = 16
TOP = 32760.0
STEP = 64.0


def encode(v):
    r = v.shape[0]
    v3 = v.reshape(r // 16, 16, LANES)
    top = jnp.maximum(jnp.max(jnp.abs(v3), axis=0), 2.0**-110)
    e = jnp.ceil(jnp.log2(top) * STEP)
    inv = jnp.exp2(e * (-1.0 / STEP)) * TOP
    code = jnp.round(v3 * inv[None]).astype(jnp.int32).reshape(r, LANES)
    return jnp.concatenate([code, e.astype(jnp.int32)], axis=0).astype(I16)


def decode(q):
    r = q.shape[0] - 16
    w = q.astype(jnp.int32).astype(F32)
    scale = jnp.exp2(w[r:] * (1.0 / STEP)) * (1.0 / TOP)
    return (w[:r].reshape(r // 16, 16, LANES) * scale[None]).reshape(r, LANES)


def kernel(
    slab,
    tiles,
    press_hbm,
    modes_hbm,
    out,
    press,
    modes,
    perm,
    sendb,
    recvb,
    bt,
    xs,
    xr,
    acc,
    ys,
    yr,
    own,
    idx,
    load_sem,
    m_send,
    m_recv,
    a_send,
    a_recv,
    x_send,
    x_recv,
    y_send,
    y_recv,
):
    mode = lax.axis_index("mode")
    resp = lax.axis_index("resp")
    core = lax.axis_index("dof")
    me = mode * 2 + core
    x = lax.rem(mode, 4)
    yh = mode // 4
    barrier = pltpu.get_barrier_semaphore()

    def greet(k, carry):
        d = lax.rem(me + k, GROUP)
        pl.semaphore_signal(
            barrier, inc=1, device_id={"mode": d // 2, "dof": lax.rem(d, 2)}
        )
        return carry

    load_p = pltpu.make_async_copy(press_hbm, press, load_sem.at[0])
    load_p.start()
    load_m = pltpu.make_async_copy(modes_hbm, modes.at[core], load_sem.at[1])
    load_m.start()
    lax.fori_loop(1, GROUP, greet, 0)

    def search(d, carry):
        found = jnp.int32(0)
        for j in range(GROUP):
            v = slab[d * GROUP + j]
            found = jnp.where(v // GROUP == me, lax.rem(v, GROUP), found)
        idx[d] = found
        return carry

    lax.fori_loop(0, GROUP, search, 0)
    load_p.wait()

    row = lax.broadcasted_iota(jnp.int32, (96, 96), 0)
    col = lax.broadcasted_iota(jnp.int32, (96, 96), 1)
    hit = jnp.zeros((96, 96), F32)
    for q in range(4):
        i = row - q * BROWS
        hit = hit + jnp.where((i >= 0) & (i < BROWS) & (col == 4 * i + q), 1.0, 0.0)
    pick = hit.astype(BF16)

    def pack(m, carry):
        parts = [
            jnp.dot(pick, press[idx[2 * m + g]], preferred_element_type=F32)
            for g in range(2)
        ]
        for h in range(2):
            for p in range(2):
                q = (h * 2 + p) * BROWS
                sendb[h, 2 * m + p] = jnp.concatenate(
                    [part[q : q + BROWS] for part in parts], axis=0
                ).astype(BF16)
        return carry

    lax.fori_loop(0, CHIPS, pack, 0)
    pl.semaphore_wait(barrier, GROUP - 1)

    for h in range(2):

        def send(k, carry):
            d = lax.rem(me + k, GROUP)
            pltpu.make_async_remote_copy(
                src_ref=sendb.at[h, d],
                dst_ref=recvb.at[h, GROUP - k],
                send_sem=a_send.at[h],
                recv_sem=a_recv.at[h],
                device_id={"mode": d // 2, "dof": lax.rem(d, 2)},
            ).start()
            return carry

        lax.fori_loop(1, GROUP, send, 0)
        if h == 0:
            swap = pltpu.make_async_remote_copy(
                src_ref=modes_hbm,
                dst_ref=modes.at[core],
                send_sem=m_send,
                recv_sem=m_recv,
                device_id={"dof": 1 - core},
            )
            swap.start()
    for h in range(2):
        recvb[h, 0] = sendb[h, me]

    load_m.wait()
    swap.wait()

    def permute(k, carry):
        s = lax.rem(me + k, GROUP)
        at = [jnp.int32(0), jnp.int32(0)]
        for g in range(2):
            for j in range(GROUP):
                v = slab[(2 * mode + g) * GROUP + j]
                at[g] = jnp.where(v // GROUP == s, j, at[g])
        for a in range(CHIPS):
            lanes = pl.ds(a * LANES, LANES)
            perm[a, k] = jnp.concatenate(
                [modes[g, at[g], :, lanes].astype(F32) for g in range(2)], axis=0
            ).astype(BF16)
        return carry

    lax.fori_loop(0, GROUP, permute, 0)

    def x_copy(h, t):
        return pltpu.make_async_remote_copy(
            src_ref=xs.at[h, t],
            dst_ref=xr.at[h, t],
            send_sem=x_send.at[h, t],
            recv_sem=x_recv.at[h, t],
            device_id={"mode": yh * 4 + lax.rem(x + (2, 1, 3)[t], 4)},
        )

    def y_target(k):
        return {
            "mode": lax.rem(yh + k // 2, 4) * 4 + x,
            "dof": lax.rem(core + lax.rem(k, 2), 2),
        }

    def first_stage(h):
        pltpu.make_async_copy(
            recvb.at[h, pl.ds(1, GROUP - 1)],
            recvb.at[h, pl.ds(1, GROUP - 1)],
            a_recv.at[h],
        ).wait()
        bt[...] = recvb[h].reshape(GROUP * 2 * BROWS, LANES).T
        for t, o in enumerate((2, 1, 3, 0)):
            xt = lax.rem(x + o, 4)

            def block(u, carry):
                both = jnp.concatenate(
                    [
                        perm[(2 * u + w) * 4 + xt].reshape(GROUP * 2 * BROWS, LANES)
                        for w in range(2)
                    ],
                    axis=1,
                )
                part = jnp.dot(bt[...], both, preferred_element_type=F32)
                for w in range(2):
                    v = part[:, w * LANES : (w + 1) * LANES]
                    if t == 3:
                        acc[h, 2 * u + w] = v
                    else:
                        xs[h, t, 2 * u + w] = encode(v)
                return carry

            lax.fori_loop(0, 2, block, 0)
            if t < 3:
                x_copy(h, t).start()

    def second_stage(h):
        for t in range(3):
            x_copy(h, t).wait_recv()

        def block(j, carry):
            yt = lax.rem(yh + j, 4)
            total = acc[h, yt]
            for t in range(3):
                total = total + decode(xr[h, t, yt])
            turned = total.T
            for w in range(2):
                half = turned[64 * w : 64 * w + 64]
                ys[h, j, w] = encode(half)
                own[h, j, w] = half
            return carry

        lax.fori_loop(0, 4, block, 0)

        def send(k, carry):
            to = y_target(k)
            pltpu.make_async_remote_copy(
                src_ref=ys.at[h, k // 2, to["dof"]],
                dst_ref=yr.at[h, k],
                send_sem=y_send.at[h],
                recv_sem=y_recv.at[h],
                device_id=to,
            ).start()
            return carry

        lax.fori_loop(1, 8, send, 0)

    def third_stage(h):
        pltpu.make_async_copy(
            yr.at[h, pl.ds(1, 7)], yr.at[h, pl.ds(1, 7)], y_recv.at[h]
        ).wait()
        same = own[h, 0, core]
        other = decode(yr[h, 1])
        for k in range(1, 4):
            same = same + decode(yr[h, 2 * k])
            other = other + decode(yr[h, 2 * k + 1])
        mine = tiles[0:1, :] == mode
        lane = lax.broadcasted_iota(jnp.int32, (64, LANES), 1)
        keep = []
        for b in range(2):
            match = mine & (tiles[1:2, :] == resp * 4 + 2 * h + b)
            keep.append(
                jnp.max(jnp.where(match, 1.0, 0.0), axis=1, keepdims=True)
            )
        mask = jnp.where(lane < 64, keep[0], keep[1])
        same = same * mask
        other = other * mask
        out[pl.ds(2 * h, 64, stride=4), :] = jnp.where(core == 0, same, other)
        out[pl.ds(2 * h + 1, 64, stride=4), :] = jnp.where(core == 0, other, same)

    first_stage(0)
    second_stage(0)
    first_stage(1)
    second_stage(1)
    for h in range(2):
        third_stage(h)

    for h in range(2):
        pltpu.make_async_copy(
            recvb.at[h, pl.ds(1, GROUP - 1)],
            recvb.at[h, pl.ds(1, GROUP - 1)],
            a_send.at[h],
        ).wait()
        for t in range(3):
            x_copy(h, t).wait_send()
        pltpu.make_async_copy(
            yr.at[h, pl.ds(1, 7)], yr.at[h, pl.ds(1, 7)], y_send.at[h]
        ).wait()


def on_device(modes, pressure, tile_list, slab_map):
    rows = pressure.shape[0]
    blocks = rows // BROWS
    press = (
        pressure.reshape(rows, 2, 2, LANES)
        .transpose(0, 2, 1, 3)
        .reshape(blocks, 4 * BROWS, LANES)
    )
    dma = pltpu.SemaphoreType.DMA
    wide = modes.shape[1]
    out = pl.pallas_call(
        kernel,
        out_shape=jax.ShapeDtypeStruct((256, LANES), F32),
        in_specs=[
            pl.BlockSpec(memory_space=pltpu.SMEM),
            pl.BlockSpec(memory_space=pltpu.VMEM),
            pl.BlockSpec(memory_space=pl.ANY),
            pl.BlockSpec(memory_space=pl.ANY),
        ],
        out_specs=pl.BlockSpec(memory_space=pltpu.VMEM),
        scratch_shapes=[
            pltpu.VMEM((blocks, 4 * BROWS, LANES), BF16),
            pltpu.VMEM((2, blocks, BROWS, wide), BF16),
            pltpu.VMEM((CHIPS, GROUP, 2 * BROWS, LANES), BF16),
            pltpu.VMEM((2, GROUP, 2 * BROWS, LANES), BF16),
            pltpu.VMEM((2, GROUP, 2 * BROWS, LANES), BF16),
            pltpu.VMEM((LANES, GROUP * 2 * BROWS), BF16),
            pltpu.VMEM((2, 3, 4, 144, LANES), I16),
            pltpu.VMEM((2, 3, 4, 144, LANES), I16),
            pltpu.VMEM((2, 4, LANES, LANES), F32),
            pltpu.VMEM((2, 4, 2, 80, LANES), I16),
            pltpu.VMEM((2, 8, 80, LANES), I16),
            pltpu.VMEM((2, 4, 2, 64, LANES), F32),
            pltpu.SMEM((GROUP,), jnp.int32),
            dma((2,)),
            dma,
            dma,
            dma((2,)),
            dma((2,)),
            dma((2, 3)),
            dma((2, 3)),
            dma((2,)),
            dma((2,)),
        ],
        compiler_params=pltpu.CompilerParams(
            collective_id=0, has_side_effects=True, vmem_limit_bytes=40 << 20
        ),
        name="forces",
    )(
        slab_map,
        tile_list.T,
        press,
        modes.reshape(blocks, BROWS, wide),
    )
    return (
        out.reshape(64, 2, 2, LANES).transpose(0, 2, 1, 3).reshape(64, 2, 2 * LANES)
    )


def solution(mesh):
    return jax.shard_map(
        on_device,
        mesh=mesh,
        in_specs=(P(("mode", "dof"), None), P(("mode", "dof"), None, "resp"), P(), P()),
        out_specs=P(("mode", "dof"), None, "resp"),
        check_vma=False,
    )
```

```python
import functools

import jax
import jax.numpy as jnp
from jax import lax
from jax.experimental import pallas as pl
from jax.experimental.pallas import tpu as pltpu
from jax.sharding import PartitionSpec as P

F32 = jnp.float32
BF16 = jnp.bfloat16
I16 = jnp.int16
LANES = 128
BROWS = 24
GROUP = 32
CHIPS = 16
TOP = 32760.0
STEP = 64.0


def encode(v):
    r = v.shape[0]
    v3 = v.reshape(r // 16, 16, LANES)
    top = jnp.maximum(jnp.max(jnp.abs(v3), axis=0), 2.0**-110)
    e = jnp.ceil(jnp.log2(top) * STEP)
    inv = jnp.exp2(e * (-1.0 / STEP)) * TOP
    code = jnp.round(v3 * inv[None]).astype(jnp.int32).reshape(r, LANES)
    return jnp.concatenate([code, e.astype(jnp.int32)], axis=0).astype(I16)


def decode(q):
    r = q.shape[0] - 16
    w = q.astype(jnp.int32).astype(F32)
    scale = jnp.exp2(w[r:] * (1.0 / STEP)) * (1.0 / TOP)
    return (w[:r].reshape(r // 16, 16, LANES) * scale[None]).reshape(r, LANES)


def kernel(
    slab_hbm,
    slabv_hbm,
    tiles_hbm,
    press_hbm,
    modes_hbm,
    out,
    slab,
    slabv,
    found,
    table,
    tiles,
    press,
    modes,
    bal,
    sendb,
    recv0,
    recv1,
    bt,
    xs,
    xr,
    acc,
    ys,
    yr,
    own,
    pick,
    load_sem,
    m_send,
    m_recv,
    a_send,
    a_recv,
    x_send,
    x_recv,
    y_send,
    y_recv,
):
    mode = lax.axis_index("mode")
    resp = lax.axis_index("resp")
    core = lax.axis_index("dof")
    me = mode * 2 + core
    x = lax.rem(mode, 4)
    yh = mode // 4
    barrier = pltpu.get_barrier_semaphore()

    def greet(k, carry):
        d = lax.rem(me + k, GROUP)
        pl.semaphore_signal(
            barrier, inc=1, device_id={"mode": d // 2, "dof": lax.rem(d, 2)}
        )
        return carry

    load_v = pltpu.make_async_copy(slabv_hbm, slabv, load_sem.at[4])
    load_v.start()
    load_s = pltpu.make_async_copy(slab_hbm, slab, load_sem.at[2])
    load_s.start()
    load_p = pltpu.make_async_copy(press_hbm, press, load_sem.at[0])
    load_p.start()
    load_m = pltpu.make_async_copy(modes_hbm, modes.at[core], load_sem.at[1])
    load_m.start()
    load_t = pltpu.make_async_copy(tiles_hbm, tiles, load_sem.at[3])
    load_t.start()
    lax.fori_loop(1, GROUP, greet, 0)

    load_v.wait()
    ids = slabv[...]
    local = jnp.where(ids // GROUP == me, lax.rem(ids, GROUP), 0)
    for shift in (1, 2, 4, 8, 16):
        local = local + pltpu.roll(local, LANES - shift, 1)
    found[...] = lax.rem(local, GROUP)
    to_smem = pltpu.make_async_copy(found, table, load_sem.at[5])
    to_smem.start()

    row = lax.broadcasted_iota(jnp.int32, (96, 96), 0)
    col = lax.broadcasted_iota(jnp.int32, (96, 96), 1)
    hit = jnp.zeros((96, 96), F32)
    for q in range(4):
        i = row - q * BROWS
        hit = hit + jnp.where((i >= 0) & (i < BROWS) & (col == 4 * i + q), 1.0, 0.0)
    pick[...] = hit.astype(BF16)

    def a_copy(h, d):
        return pltpu.make_async_remote_copy(
            src_ref=sendb.at[h, d],
            dst_ref=(recv0, recv1)[h].at[lax.rem(me - d + GROUP, GROUP)],
            send_sem=a_send.at[h],
            recv_sem=a_recv.at[h],
            device_id={"mode": d // 2, "dof": lax.rem(d, 2)},
        )

    def a_wait(sem):
        part = recv0.at[pl.ds(1, GROUP - 1)]
        pltpu.make_async_copy(part, part, sem).wait()

    load_s.wait()
    load_p.wait()
    to_smem.wait()
    pl.semaphore_wait(barrier, GROUP - 1)
    swap = pltpu.make_async_remote_copy(
        src_ref=modes_hbm,
        dst_ref=modes.at[core],
        send_sem=m_send,
        recv_sem=m_recv,
        device_id={"dof": 1 - core},
    )
    swap.start()

    def pack(m):
        parts = []
        for g in range(2):
            d = 2 * m + g
            block = press[table[d // 4, GROUP * lax.rem(d, 4)]]
            parts.append(jnp.dot(pick[...], block, preferred_element_type=F32))
        for h in range(2):
            for p in range(2):
                q = (h * 2 + p) * BROWS
                sendb[h, 2 * m + p] = jnp.concatenate(
                    [part[q : q + BROWS] for part in parts], axis=0
                ).astype(BF16)

    def chip(k):
        r = lax.rem(k, 3)
        step = jnp.where(r == 0, 2, jnp.where(r == 1, 1, 3))
        far = k < 12
        dy = jnp.where(far, step, 0)
        dx = jnp.where(far, k // 3, step)
        return lax.rem(yh + dy, 4) * 4 + lax.rem(x + dx, 4)

    def pack_and_send(k, carry):
        m = chip(k)
        pack(m)
        for p in range(2):
            a_copy(0, 2 * m + p).start()
        return carry

    lax.fori_loop(0, CHIPS - 1, pack_and_send, 0, unroll=3)
    pack(mode)
    mate = mode * 2 + 1 - core
    recv0[0] = sendb[0, me]
    recv1[0] = sendb[1, me]
    a_copy(0, mate).start()

    a_wait(a_send.at[0])

    def send(k, carry):
        for p in range(2):
            a_copy(1, 2 * chip(k) + p).start()
        return carry

    lax.fori_loop(0, CHIPS - 1, send, 0)
    a_copy(1, mate).start()
    load_m.wait()
    swap.wait()

    def across(t):
        return jnp.where(t == 0, 2, jnp.where(t == 1, 1, jnp.where(t == 2, 3, 0)))

    def x_copy(h, t):
        return pltpu.make_async_remote_copy(
            src_ref=xs.at[h, t],
            dst_ref=xr.at[h, t],
            send_sem=x_send.at[h, t],
            recv_sem=x_recv.at[h, t],
            device_id={"mode": yh * 4 + lax.rem(x + across(t), 4)},
        )

    def y_wait(sem):
        part = yr.at[0, pl.ds(1, 7)]
        pltpu.make_async_copy(part, part, sem).wait()

    def first_stage(h):
        a_wait(a_recv.at[h])

        def align(recv, i, carry):
            for g in range(2):
                parts = []
                for w in range(2):
                    q = slab[(2 * mode + g) * GROUP + 2 * i + w] // GROUP
                    slot = lax.rem(q - me + GROUP, GROUP)
                    both = recv[slot].astype(F32)
                    parts.append(both[g * BROWS : (g + 1) * BROWS])
                bal[g, i] = jnp.concatenate(parts, axis=0).astype(BF16)
            return carry

        for way, recv in enumerate((recv0, recv1)):

            @pl.when(h == way)
            def _():
                lax.fori_loop(0, GROUP // 2, functools.partial(align, recv), 0)

        bt[...] = bal[...].reshape(GROUP * 2 * BROWS, LANES).T

        def block(n, carry):
            t = n // 2
            u = lax.rem(n, 2)
            xt = lax.rem(x + across(t), 4)
            part = jnp.zeros((LANES, 2 * LANES), F32)
            for g in range(2):
                both = jnp.concatenate(
                    [
                        modes[g, :, pl.ds(((2 * u + w) * 4 + xt) * LANES, LANES)]
                        for w in range(2)
                    ],
                    axis=1,
                )
                depth = GROUP * BROWS
                part = part + jnp.dot(
                    bt[:, g * depth : (g + 1) * depth],
                    both,
                    preferred_element_type=F32,
                )
            halves = [part[:, w * LANES : (w + 1) * LANES] for w in range(2)]

            @pl.when(t == 3)
            def _():
                for w in range(2):
                    acc[h, 2 * u + w] = halves[w]

            @pl.when(t < 3)
            def _():
                for w in range(2):
                    xs[h, t, 2 * u + w] = encode(halves[w])

                @pl.when(u == 1)
                def _():
                    x_copy(h, t).start()

            return carry

        lax.fori_loop(0, 8, block, 0)

    def second_stage(h):
        for t in range(3):
            x_copy(h, t).wait_recv()

        def block(j, carry):
            yt = lax.rem(yh + j, 4)
            total = acc[h, yt]
            for t in range(3):
                total = total + decode(xr[h, t, yt])
            turned = total.T

            @pl.when(j == 0)
            def _():
                own[h] = turned.reshape(2, 64, LANES)

            for w in range(2):
                ys[h, j, w] = encode(turned[64 * w : 64 * w + 64])

            def send(w, carry):
                to = lax.rem(core + w, 2)
                pltpu.make_async_remote_copy(
                    src_ref=ys.at[h, j, to],
                    dst_ref=yr.at[h, 2 * j + w],
                    send_sem=y_send.at[h],
                    recv_sem=y_recv.at[h],
                    device_id={"mode": yt * 4 + x, "dof": to},
                ).start()
                return carry

            lax.fori_loop(jnp.where(j == 0, 1, 0), 2, send, 0)
            return carry

        lax.fori_loop(0, 4, block, 0)

    def third_stage(h):
        y_wait(y_recv.at[h])
        same = own[h, core]
        other = decode(yr[h, 1])
        for k in range(1, 4):
            same = same + decode(yr[h, 2 * k])
            other = other + decode(yr[h, 2 * k + 1])
        mine = tiles[0:1, :] == mode
        lane = lax.broadcasted_iota(jnp.int32, (64, LANES), 1)
        keep = []
        for b in range(2):
            match = mine & (tiles[1:2, :] == resp * 4 + 2 * h + b)
            keep.append(jnp.max(jnp.where(match, 1.0, 0.0), axis=1, keepdims=True))
        mask = jnp.where(lane < 64, keep[0], keep[1])
        same = same * mask
        other = other * mask
        out[pl.ds(2 * h, 64, stride=4), :] = jnp.where(core == 0, same, other)
        out[pl.ds(2 * h + 1, 64, stride=4), :] = jnp.where(core == 0, other, same)

    def first(h, carry):
        first_stage(h)
        return carry

    def second(h, carry):
        second_stage(h)
        return carry

    def third(h, carry):
        third_stage(h)
        return carry

    lax.fori_loop(0, 2, first, 0)
    lax.fori_loop(0, 2, second, 0)
    load_t.wait()
    lax.fori_loop(0, 2, third, 0)

    a_wait(a_send.at[1])
    for h in range(2):
        for t in range(3):
            x_copy(h, t).wait_send()
        y_wait(y_send.at[h])


def on_device(modes, pressure, tile_list, slab_map):
    rows = pressure.shape[0]
    blocks = rows // BROWS
    press = (
        pressure.reshape(rows, 2, 2, LANES)
        .transpose(0, 2, 1, 3)
        .reshape(blocks, 4 * BROWS, LANES)
    )
    dma = pltpu.SemaphoreType.DMA
    wide = modes.shape[1]
    out = pl.pallas_call(
        kernel,
        out_shape=jax.ShapeDtypeStruct((256, LANES), F32),
        in_specs=[
            pl.BlockSpec(memory_space=pltpu.HBM),
            pl.BlockSpec(memory_space=pltpu.HBM),
            pl.BlockSpec(memory_space=pltpu.HBM),
            pl.BlockSpec(memory_space=pltpu.HBM),
            pl.BlockSpec(memory_space=pltpu.HBM),
        ],
        out_specs=pl.BlockSpec(memory_space=pltpu.VMEM),
        scratch_shapes=[
            pltpu.SMEM(slab_map.shape, jnp.int32),
            pltpu.VMEM((8, LANES), jnp.int32),
            pltpu.VMEM((8, LANES), jnp.int32),
            pltpu.SMEM((8, LANES), jnp.int32),
            pltpu.VMEM(tile_list.shape[::-1], jnp.int32),
            pltpu.VMEM((blocks, 4 * BROWS, LANES), BF16),
            pltpu.VMEM((2, rows, wide), BF16),
            pltpu.VMEM((2, blocks // 2, 2 * BROWS, LANES), BF16),
            pltpu.VMEM((2, GROUP, 2 * BROWS, LANES), BF16),
            pltpu.VMEM((GROUP, 2 * BROWS, LANES), BF16),
            pltpu.VMEM((GROUP, 2 * BROWS, LANES), BF16),
            pltpu.VMEM((LANES, GROUP * 2 * BROWS), BF16),
            pltpu.VMEM((2, 3, 4, 144, LANES), I16),
            pltpu.VMEM((2, 3, 4, 144, LANES), I16),
            pltpu.VMEM((2, 4, LANES, LANES), F32),
            pltpu.VMEM((2, 4, 2, 80, LANES), I16),
            pltpu.VMEM((2, 8, 80, LANES), I16),
            pltpu.VMEM((2, 2, 64, LANES), F32),
            pltpu.VMEM((96, 96), BF16),
            dma((6,)),
            dma,
            dma,
            dma((2,)),
            dma((2,)),
            dma((2, 3)),
            dma((2, 3)),
            dma((2,)),
            dma((2,)),
        ],
        compiler_params=pltpu.CompilerParams(
            collective_id=0, has_side_effects=True, vmem_limit_bytes=60 << 20
        ),
        name="forces",
    )(
        slab_map,
        slab_map.reshape(8, LANES),
        tile_list.T,
        press,
        modes,
    )
    return (
        out.reshape(64, 2, 2, LANES).transpose(0, 2, 1, 3).reshape(64, 2, 2 * LANES)
    )


def solution(mesh):
    return jax.shard_map(
        on_device,
        mesh=mesh,
        in_specs=(P(("mode", "dof"), None), P(("mode", "dof"), None, "resp"), P(), P()),
        out_specs=P(("mode", "dof"), None, "resp"),
        check_vma=False,
    )
```

```python
import functools

import jax
import jax.numpy as jnp
from jax import lax
from jax.experimental import pallas as pl
from jax.experimental.pallas import tpu as pltpu
from jax.sharding import PartitionSpec as P

F32 = jnp.float32
BF16 = jnp.bfloat16
I16 = jnp.int16
LANES = 128
BROWS = 24
GROUP = 32
CHIPS = 16
TOP = 32760.0
STEP = 64.0


def encode(v):
    r = v.shape[0]
    v3 = v.reshape(r // 16, 16, LANES)
    top = jnp.maximum(jnp.max(jnp.abs(v3), axis=0), 2.0**-110)
    e = jnp.ceil(jnp.log2(top) * STEP)
    inv = jnp.exp2(e * (-1.0 / STEP)) * TOP
    code = jnp.round(v3 * inv[None]).astype(jnp.int32).reshape(r, LANES)
    return jnp.concatenate([code, e.astype(jnp.int32)], axis=0).astype(I16)


def decode(q):
    r = q.shape[0] - 16
    w = q.astype(jnp.int32).astype(F32)
    scale = jnp.exp2(w[r:] * (1.0 / STEP)) * (1.0 / TOP)
    return (w[:r].reshape(r // 16, 16, LANES) * scale[None]).reshape(r, LANES)


def kernel(
    slab_hbm,
    slabv_hbm,
    tiles_hbm,
    press_hbm,
    modes_hbm,
    out,
    slab,
    slabv,
    found,
    table,
    tiles,
    press,
    modes,
    bal,
    sendb,
    recv0,
    recv1,
    bt,
    xs,
    xr,
    acc,
    ys,
    yr,
    own,
    pick,
    load_sem,
    m_send,
    m_recv,
    a_send,
    a_recv,
    x_send,
    x_recv,
    y_send,
    y_recv,
):
    mode = lax.axis_index("mode")
    resp = lax.axis_index("resp")
    core = lax.axis_index("dof")
    me = mode * 2 + core
    x = lax.rem(mode, 4)
    yh = mode // 4
    barrier = pltpu.get_barrier_semaphore()

    def greet(k, carry):
        d = lax.rem(me + k, GROUP)
        pl.semaphore_signal(
            barrier, inc=1, device_id={"mode": d // 2, "dof": lax.rem(d, 2)}
        )
        return carry

    load_v = pltpu.make_async_copy(slabv_hbm, slabv, load_sem.at[4])
    load_v.start()
    load_s = pltpu.make_async_copy(slab_hbm, slab, load_sem.at[2])
    load_s.start()
    load_p = pltpu.make_async_copy(press_hbm, press, load_sem.at[0])
    load_p.start()
    load_m = pltpu.make_async_copy(modes_hbm, modes.at[core], load_sem.at[1])
    load_m.start()
    load_t = pltpu.make_async_copy(tiles_hbm, tiles, load_sem.at[3])
    load_t.start()
    lax.fori_loop(1, GROUP, greet, 0)

    load_v.wait()
    ids = slabv[...]
    local = jnp.where(ids // GROUP == me, lax.rem(ids, GROUP), 0)
    for shift in (1, 2, 4, 8, 16):
        local = local + pltpu.roll(local, LANES - shift, 1)
    found[...] = lax.rem(local, GROUP)
    to_smem = pltpu.make_async_copy(found, table, load_sem.at[5])
    to_smem.start()

    row = lax.broadcasted_iota(jnp.int32, (96, 96), 0)
    col = lax.broadcasted_iota(jnp.int32, (96, 96), 1)
    hit = jnp.zeros((96, 96), F32)
    for q in range(4):
        i = row - q * BROWS
        hit = hit + jnp.where((i >= 0) & (i < BROWS) & (col == 4 * i + q), 1.0, 0.0)
    pick[...] = hit.astype(BF16)

    def a_copy(h, d):
        return pltpu.make_async_remote_copy(
            src_ref=sendb.at[h, d],
            dst_ref=(recv0, recv1)[h].at[lax.rem(me - d + GROUP, GROUP)],
            send_sem=a_send.at[h],
            recv_sem=a_recv.at[h],
            device_id={"mode": d // 2, "dof": lax.rem(d, 2)},
        )

    def a_wait(sem):
        part = recv0.at[pl.ds(1, GROUP - 1)]
        pltpu.make_async_copy(part, part, sem).wait()

    load_s.wait()
    load_p.wait()
    to_smem.wait()
    pl.semaphore_wait(barrier, GROUP - 1)
    swap = pltpu.make_async_remote_copy(
        src_ref=modes_hbm,
        dst_ref=modes.at[core],
        send_sem=m_send,
        recv_sem=m_recv,
        device_id={"dof": 1 - core},
    )
    swap.start()

    def pack(m):
        parts = []
        for g in range(2):
            d = 2 * m + g
            block = press[table[d // 4, GROUP * lax.rem(d, 4)]]
            parts.append(jnp.dot(pick[...], block, preferred_element_type=F32))
        for h in range(2):
            for p in range(2):
                q = (h * 2 + p) * BROWS
                sendb[h, 2 * m + p] = jnp.concatenate(
                    [part[q : q + BROWS] for part in parts], axis=0
                ).astype(BF16)

    def chip(k):
        r = lax.rem(k, 3)
        step = jnp.where(r == 0, 2, jnp.where(r == 1, 1, 3))
        far = k < 12
        dy = jnp.where(far, step, 0)
        dx = jnp.where(far, k // 3, step)
        return lax.rem(yh + dy, 4) * 4 + lax.rem(x + dx, 4)

    def pack_and_send(k, carry):
        m = chip(k)
        pack(m)
        for p in range(2):
            a_copy(0, 2 * m + p).start()
        return carry

    lax.fori_loop(0, CHIPS - 1, pack_and_send, 0, unroll=3)
    pack(mode)
    mate = mode * 2 + 1 - core
    recv0[0] = sendb[0, me]
    recv1[0] = sendb[1, me]
    a_copy(0, mate).start()

    def send(k, carry):
        for p in range(2):
            a_copy(1, 2 * chip(k) + p).start()
        return carry

    lax.fori_loop(0, CHIPS - 1, send, 0)
    a_copy(1, mate).start()
    load_m.wait()
    swap.wait()

    def across(t):
        return jnp.where(t == 0, 2, jnp.where(t == 1, 1, jnp.where(t == 2, 3, 0)))

    def x_copy(h, t, u):
        return pltpu.make_async_remote_copy(
            src_ref=xs.at[h, t, u],
            dst_ref=xr.at[h, t, u],
            send_sem=x_send.at[h, t, u],
            recv_sem=x_recv.at[h, t, u],
            device_id={"mode": yh * 4 + lax.rem(x + across(t), 4)},
        )

    def y_wait(sem):
        part = yr.at[0, pl.ds(1, 7)]
        pltpu.make_async_copy(part, part, sem).wait()

    def first_stage(h):
        a_wait(a_recv.at[h])

        def align(recv, i, carry):
            for g in range(2):
                parts = []
                for w in range(2):
                    q = slab[(2 * mode + g) * GROUP + 2 * i + w] // GROUP
                    slot = lax.rem(q - me + GROUP, GROUP)
                    both = recv[slot].astype(F32)
                    parts.append(both[g * BROWS : (g + 1) * BROWS])
                bal[g, i] = jnp.concatenate(parts, axis=0).astype(BF16)
            return carry

        for way, recv in enumerate((recv0, recv1)):

            @pl.when(h == way)
            def _():
                lax.fori_loop(0, GROUP // 2, functools.partial(align, recv), 0)

        bt[...] = bal[...].reshape(GROUP * 2 * BROWS, LANES).T

        def block(n, carry):
            u = n // 4
            t = lax.rem(n, 4)
            xt = lax.rem(x + across(t), 4)
            part = jnp.zeros((LANES, 2 * LANES), F32)
            for g in range(2):
                both = jnp.concatenate(
                    [
                        modes[g, :, pl.ds(((2 * u + w) * 4 + xt) * LANES, LANES)]
                        for w in range(2)
                    ],
                    axis=1,
                )
                depth = GROUP * BROWS
                part = part + jnp.dot(
                    bt[:, g * depth : (g + 1) * depth],
                    both,
                    preferred_element_type=F32,
                )
            halves = [part[:, w * LANES : (w + 1) * LANES] for w in range(2)]

            @pl.when(t == 3)
            def _():
                for w in range(2):
                    acc[h, 2 * u + w] = halves[w]

            @pl.when(t < 3)
            def _():
                for w in range(2):
                    xs[h, t, u, w] = encode(halves[w])
                x_copy(h, t, u).start()

            return carry

        lax.fori_loop(0, 8, block, 0)

    def second_stage(h, u):
        for t in range(3):
            x_copy(h, t, u).wait_recv()

        def block(v, carry):
            yt = 2 * u + v
            j = lax.rem(yt - yh + 4, 4)
            total = acc[h, yt]
            for t in range(3):
                total = total + decode(xr[h, t, u, v])
            turned = total.T

            @pl.when(j == 0)
            def _():
                own[h] = turned.reshape(2, 64, LANES)

            for w in range(2):
                ys[h, j, w] = encode(turned[64 * w : 64 * w + 64])

            def send(w, carry):
                to = lax.rem(core + w, 2)
                pltpu.make_async_remote_copy(
                    src_ref=ys.at[h, j, to],
                    dst_ref=yr.at[h, 2 * j + w],
                    send_sem=y_send.at[h],
                    recv_sem=y_recv.at[h],
                    device_id={"mode": yt * 4 + x, "dof": to},
                ).start()
                return carry

            lax.fori_loop(jnp.where(j == 0, 1, 0), 2, send, 0)
            return carry

        lax.fori_loop(0, 2, block, 0)

    def third_stage(h):
        y_wait(y_recv.at[h])
        same = own[h, core]
        other = decode(yr[h, 1])
        for k in range(1, 4):
            same = same + decode(yr[h, 2 * k])
            other = other + decode(yr[h, 2 * k + 1])
        mine = tiles[0:1, :] == mode
        lane = lax.broadcasted_iota(jnp.int32, (64, LANES), 1)
        keep = []
        for b in range(2):
            match = mine & (tiles[1:2, :] == resp * 4 + 2 * h + b)
            keep.append(jnp.max(jnp.where(match, 1.0, 0.0), axis=1, keepdims=True))
        mask = jnp.where(lane < 64, keep[0], keep[1])
        same = same * mask
        other = other * mask
        out[pl.ds(2 * h, 64, stride=4), :] = jnp.where(core == 0, same, other)
        out[pl.ds(2 * h + 1, 64, stride=4), :] = jnp.where(core == 0, other, same)

    def first(h, carry):
        first_stage(h)
        return carry

    def second(n, carry):
        second_stage(n // 2, lax.rem(n, 2))
        return carry

    def third(h, carry):
        third_stage(h)
        return carry

    lax.fori_loop(0, 2, first, 0)
    lax.fori_loop(0, 4, second, 0)
    load_t.wait()
    lax.fori_loop(0, 2, third, 0)

    a_wait(a_send.at[0])
    a_wait(a_send.at[1])
    for h in range(2):
        for t in range(3):
            for u in range(2):
                x_copy(h, t, u).wait_send()
        y_wait(y_send.at[h])


def on_device(modes, pressure, tile_list, slab_map):
    rows = pressure.shape[0]
    blocks = rows // BROWS
    press = (
        pressure.reshape(rows, 2, 2, LANES)
        .transpose(0, 2, 1, 3)
        .reshape(blocks, 4 * BROWS, LANES)
    )
    dma = pltpu.SemaphoreType.DMA
    wide = modes.shape[1]
    out = pl.pallas_call(
        kernel,
        out_shape=jax.ShapeDtypeStruct((256, LANES), F32),
        in_specs=[
            pl.BlockSpec(memory_space=pltpu.HBM),
            pl.BlockSpec(memory_space=pltpu.HBM),
            pl.BlockSpec(memory_space=pltpu.HBM),
            pl.BlockSpec(memory_space=pltpu.HBM),
            pl.BlockSpec(memory_space=pltpu.HBM),
        ],
        out_specs=pl.BlockSpec(memory_space=pltpu.VMEM),
        scratch_shapes=[
            pltpu.SMEM(slab_map.shape, jnp.int32),
            pltpu.VMEM((8, LANES), jnp.int32),
            pltpu.VMEM((8, LANES), jnp.int32),
            pltpu.SMEM((8, LANES), jnp.int32),
            pltpu.VMEM(tile_list.shape[::-1], jnp.int32),
            pltpu.VMEM((blocks, 4 * BROWS, LANES), BF16),
            pltpu.VMEM((2, rows, wide), BF16),
            pltpu.VMEM((2, blocks // 2, 2 * BROWS, LANES), BF16),
            pltpu.VMEM((2, GROUP, 2 * BROWS, LANES), BF16),
            pltpu.VMEM((GROUP, 2 * BROWS, LANES), BF16),
            pltpu.VMEM((GROUP, 2 * BROWS, LANES), BF16),
            pltpu.VMEM((LANES, GROUP * 2 * BROWS), BF16),
            pltpu.VMEM((2, 3, 2, 2, 144, LANES), I16),
            pltpu.VMEM((2, 3, 2, 2, 144, LANES), I16),
            pltpu.VMEM((2, 4, LANES, LANES), F32),
            pltpu.VMEM((2, 4, 2, 80, LANES), I16),
            pltpu.VMEM((2, 8, 80, LANES), I16),
            pltpu.VMEM((2, 2, 64, LANES), F32),
            pltpu.VMEM((96, 96), BF16),
            dma((6,)),
            dma,
            dma,
            dma((2,)),
            dma((2,)),
            dma((2, 3, 2)),
            dma((2, 3, 2)),
            dma((2,)),
            dma((2,)),
        ],
        compiler_params=pltpu.CompilerParams(
            collective_id=0, has_side_effects=True, vmem_limit_bytes=60 << 20
        ),
        name="forces",
    )(
        slab_map,
        slab_map.reshape(8, LANES),
        tile_list.T,
        press,
        modes,
    )
    return (
        out.reshape(64, 2, 2, LANES).transpose(0, 2, 1, 3).reshape(64, 2, 2 * LANES)
    )


def solution(mesh):
    return jax.shard_map(
        on_device,
        mesh=mesh,
        in_specs=(P(("mode", "dof"), None), P(("mode", "dof"), None, "resp"), P(), P()),
        out_specs=P(("mode", "dof"), None, "resp"),
        check_vma=False,
    )
```

```python
import functools

import jax
import jax.numpy as jnp
from jax import lax
from jax.experimental import pallas as pl
from jax.experimental.pallas import tpu as pltpu
from jax.sharding import PartitionSpec as P

F32 = jnp.float32
BF16 = jnp.bfloat16
I16 = jnp.int16
LANES = 128
BROWS = 24
GROUP = 32
CHIPS = 16
TOP = 32760.0
STEP = 64.0


def encode(v):
    r = v.shape[0]
    v3 = v.reshape(r // 16, 16, LANES)
    top = jnp.maximum(jnp.max(jnp.abs(v3), axis=0), 2.0**-110)
    e = jnp.ceil(jnp.log2(top) * STEP)
    inv = jnp.exp2(e * (-1.0 / STEP)) * TOP
    code = jnp.round(v3 * inv[None]).astype(jnp.int32).reshape(r, LANES)
    return jnp.concatenate([code, e.astype(jnp.int32)], axis=0).astype(I16)


def decode(q):
    r = q.shape[0] - 16
    w = q.astype(jnp.int32).astype(F32)
    scale = jnp.exp2(w[r:] * (1.0 / STEP)) * (1.0 / TOP)
    return (w[:r].reshape(r // 16, 16, LANES) * scale[None]).reshape(r, LANES)


def kernel(
    slab_hbm,
    slabv_hbm,
    tiles_hbm,
    press_hbm,
    modes_hbm,
    out,
    slab,
    slabv,
    found,
    table,
    tiles,
    press,
    modes,
    bal,
    sendb,
    recv0,
    recv1,
    bt,
    xs,
    xr,
    acc,
    ys,
    yr,
    own,
    pick,
    load_sem,
    m_send,
    m_recv,
    a_send,
    a_recv,
    x_send,
    x_recv,
    y_send,
    y_recv,
):
    mode = lax.axis_index("mode")
    resp = lax.axis_index("resp")
    core = lax.axis_index("dof")
    me = mode * 2 + core
    x = lax.rem(mode, 4)
    yh = mode // 4
    barrier = pltpu.get_barrier_semaphore()

    def greet(k, carry):
        d = lax.rem(me + k, GROUP)
        pl.semaphore_signal(
            barrier, inc=1, device_id={"mode": d // 2, "dof": lax.rem(d, 2)}
        )
        return carry

    load_v = pltpu.make_async_copy(slabv_hbm, slabv, load_sem.at[4])
    load_v.start()
    load_s = pltpu.make_async_copy(slab_hbm, slab, load_sem.at[2])
    load_s.start()
    load_p = pltpu.make_async_copy(press_hbm, press, load_sem.at[0])
    load_p.start()
    load_m = pltpu.make_async_copy(modes_hbm, modes.at[core], load_sem.at[1])
    load_m.start()
    load_t = pltpu.make_async_copy(tiles_hbm, tiles, load_sem.at[3])
    load_t.start()
    lax.fori_loop(1, GROUP, greet, 0)

    load_v.wait()
    ids = slabv[...]
    local = jnp.where(ids // GROUP == me, lax.rem(ids, GROUP), 0)
    for shift in (1, 2, 4, 8, 16):
        local = local + pltpu.roll(local, LANES - shift, 1)
    found[...] = lax.rem(local, GROUP)
    to_smem = pltpu.make_async_copy(found, table, load_sem.at[5])
    to_smem.start()

    row = lax.broadcasted_iota(jnp.int32, (96, 96), 0)
    col = lax.broadcasted_iota(jnp.int32, (96, 96), 1)
    hit = jnp.zeros((96, 96), F32)
    for q in range(4):
        i = row - q * BROWS
        hit = hit + jnp.where((i >= 0) & (i < BROWS) & (col == 4 * i + q), 1.0, 0.0)
    pick[...] = hit.astype(BF16)

    def a_copy(h, d):
        return pltpu.make_async_remote_copy(
            src_ref=sendb.at[h, d],
            dst_ref=(recv0, recv1)[h].at[lax.rem(me - d + GROUP, GROUP)],
            send_sem=a_send.at[h],
            recv_sem=a_recv.at[h],
            device_id={"mode": d // 2, "dof": lax.rem(d, 2)},
        )

    def a_wait(sem):
        part = recv0.at[pl.ds(1, GROUP - 1)]
        pltpu.make_async_copy(part, part, sem).wait()

    load_s.wait()
    load_p.wait()
    to_smem.wait()
    pl.semaphore_wait(barrier, GROUP - 1)
    swap = pltpu.make_async_remote_copy(
        src_ref=modes_hbm,
        dst_ref=modes.at[core],
        send_sem=m_send,
        recv_sem=m_recv,
        device_id={"dof": 1 - core},
    )
    swap.start()

    def pack(m):
        parts = []
        for g in range(2):
            d = 2 * m + g
            block = press[table[d // 4, GROUP * lax.rem(d, 4)]]
            parts.append(jnp.dot(pick[...], block, preferred_element_type=F32))
        for h in range(2):
            for p in range(2):
                q = (h * 2 + p) * BROWS
                sendb[h, 2 * m + p] = jnp.concatenate(
                    [part[q : q + BROWS] for part in parts], axis=0
                ).astype(BF16)

    def chip(k):
        r = lax.rem(k, 3)
        step = jnp.where(r == 0, 2, jnp.where(r == 1, 1, 3))
        far = k < 12
        dy = jnp.where(far, step, 0)
        dx = jnp.where(far, lax.rem(core * 2 + k // 3, 4), step)
        return lax.rem(yh + dy, 4) * 4 + lax.rem(x + dx, 4)

    def pack_and_send(k, carry):
        m = chip(k)
        pack(m)
        for p in range(2):
            a_copy(0, 2 * m + p).start()
        return carry

    lax.fori_loop(0, CHIPS - 1, pack_and_send, 0, unroll=3)
    pack(mode)
    mate = mode * 2 + 1 - core
    recv0[0] = sendb[0, me]
    recv1[0] = sendb[1, me]
    a_copy(0, mate).start()

    def send(k, carry):
        for p in range(2):
            a_copy(1, 2 * chip(k) + p).start()
        return carry

    lax.fori_loop(0, CHIPS - 1, send, 0)
    a_copy(1, mate).start()
    load_m.wait()
    swap.wait()

    def across(t):
        return jnp.where(t == 0, 1, jnp.where(t == 1, 3, jnp.where(t == 2, 2, 0)))

    def x_copy(h, t, u):
        return pltpu.make_async_remote_copy(
            src_ref=xs.at[h, t, u],
            dst_ref=xr.at[h, t, u],
            send_sem=x_send.at[h, t, u],
            recv_sem=x_recv.at[h, t, u],
            device_id={"mode": yh * 4 + lax.rem(x + across(t), 4)},
        )

    def y_wait(sem):
        part = yr.at[0, pl.ds(1, 7)]
        pltpu.make_async_copy(part, part, sem).wait()

    def first_stage(h):
        a_wait(a_recv.at[h])

        def align(recv, i, carry):
            for g in range(2):
                parts = []
                for w in range(2):
                    q = slab[(2 * mode + g) * GROUP + 2 * i + w] // GROUP
                    slot = lax.rem(q - me + GROUP, GROUP)
                    both = recv[slot].astype(F32)
                    parts.append(both[g * BROWS : (g + 1) * BROWS])
                bal[g, i] = jnp.concatenate(parts, axis=0).astype(BF16)
            return carry

        for way, recv in enumerate((recv0, recv1)):

            @pl.when(h == way)
            def _():
                lax.fori_loop(0, GROUP // 2, functools.partial(align, recv), 0)

        bt[...] = bal[...].reshape(GROUP * 2 * BROWS, LANES).T

        def block(n, carry):
            u = n // 4
            t = lax.rem(n, 4)
            xt = lax.rem(x + across(t), 4)
            part = jnp.zeros((LANES, 2 * LANES), F32)
            for g in range(2):
                both = jnp.concatenate(
                    [
                        modes[g, :, pl.ds(((2 * u + w) * 4 + xt) * LANES, LANES)]
                        for w in range(2)
                    ],
                    axis=1,
                )
                depth = GROUP * BROWS
                part = part + jnp.dot(
                    bt[:, g * depth : (g + 1) * depth],
                    both,
                    preferred_element_type=F32,
                )
            halves = [part[:, w * LANES : (w + 1) * LANES] for w in range(2)]

            @pl.when(t == 3)
            def _():
                for w in range(2):
                    acc[h, 2 * u + w] = halves[w]

            @pl.when(t < 3)
            def _():
                for w in range(2):
                    xs[h, t, u, w] = encode(halves[w])
                x_copy(h, t, u).start()

            return carry

        lax.fori_loop(0, 8, block, 0)

    def second_stage(h, u):
        for t in range(3):
            x_copy(h, t, u).wait_recv()

        def block(v, carry):
            yt = 2 * u + v
            j = lax.rem(yt - yh + 4, 4)
            total = acc[h, yt]
            for t in range(3):
                total = total + decode(xr[h, t, u, v])
            turned = total.T

            @pl.when(j == 0)
            def _():
                own[h] = turned.reshape(2, 64, LANES)

            for w in range(2):
                ys[h, j, w] = encode(turned[64 * w : 64 * w + 64])

            def send(w, carry):
                to = lax.rem(core + w, 2)
                pltpu.make_async_remote_copy(
                    src_ref=ys.at[h, j, to],
                    dst_ref=yr.at[h, 2 * j + w],
                    send_sem=y_send.at[h],
                    recv_sem=y_recv.at[h],
                    device_id={"mode": yt * 4 + x, "dof": to},
                ).start()
                return carry

            lax.fori_loop(jnp.where(j == 0, 1, 0), 2, send, 0)
            return carry

        lax.fori_loop(0, 2, block, 0)

    def third_stage(h):
        y_wait(y_recv.at[h])
        same = own[h, core]
        other = decode(yr[h, 1])
        for k in range(1, 4):
            same = same + decode(yr[h, 2 * k])
            other = other + decode(yr[h, 2 * k + 1])
        mine = tiles[0:1, :] == mode
        lane = lax.broadcasted_iota(jnp.int32, (64, LANES), 1)
        keep = []
        for b in range(2):
            match = mine & (tiles[1:2, :] == resp * 4 + 2 * h + b)
            keep.append(jnp.max(jnp.where(match, 1.0, 0.0), axis=1, keepdims=True))
        mask = jnp.where(lane < 64, keep[0], keep[1])
        same = same * mask
        other = other * mask
        out[pl.ds(2 * h, 64, stride=4), :] = jnp.where(core == 0, same, other)
        out[pl.ds(2 * h + 1, 64, stride=4), :] = jnp.where(core == 0, other, same)

    def first(h, carry):
        first_stage(h)
        return carry

    def second(n, carry):
        second_stage(n // 2, lax.rem(n, 2))
        return carry

    def third(h, carry):
        third_stage(h)
        return carry

    lax.fori_loop(0, 2, first, 0)
    lax.fori_loop(0, 4, second, 0)
    load_t.wait()
    lax.fori_loop(0, 2, third, 0)

    a_wait(a_send.at[0])
    a_wait(a_send.at[1])
    for h in range(2):
        for t in range(3):
            for u in range(2):
                x_copy(h, t, u).wait_send()
        y_wait(y_send.at[h])


def on_device(modes, pressure, tile_list, slab_map):
    rows = pressure.shape[0]
    blocks = rows // BROWS
    press = (
        pressure.reshape(rows, 2, 2, LANES)
        .transpose(0, 2, 1, 3)
        .reshape(blocks, 4 * BROWS, LANES)
    )
    dma = pltpu.SemaphoreType.DMA
    wide = modes.shape[1]
    out = pl.pallas_call(
        kernel,
        out_shape=jax.ShapeDtypeStruct((256, LANES), F32),
        in_specs=[
            pl.BlockSpec(memory_space=pltpu.HBM),
            pl.BlockSpec(memory_space=pltpu.HBM),
            pl.BlockSpec(memory_space=pltpu.HBM),
            pl.BlockSpec(memory_space=pltpu.HBM),
            pl.BlockSpec(memory_space=pltpu.HBM),
        ],
        out_specs=pl.BlockSpec(memory_space=pltpu.VMEM),
        scratch_shapes=[
            pltpu.SMEM(slab_map.shape, jnp.int32),
            pltpu.VMEM((8, LANES), jnp.int32),
            pltpu.VMEM((8, LANES), jnp.int32),
            pltpu.SMEM((8, LANES), jnp.int32),
            pltpu.VMEM(tile_list.shape[::-1], jnp.int32),
            pltpu.VMEM((blocks, 4 * BROWS, LANES), BF16),
            pltpu.VMEM((2, rows, wide), BF16),
            pltpu.VMEM((2, blocks // 2, 2 * BROWS, LANES), BF16),
            pltpu.VMEM((2, GROUP, 2 * BROWS, LANES), BF16),
            pltpu.VMEM((GROUP, 2 * BROWS, LANES), BF16),
            pltpu.VMEM((GROUP, 2 * BROWS, LANES), BF16),
            pltpu.VMEM((LANES, GROUP * 2 * BROWS), BF16),
            pltpu.VMEM((2, 3, 2, 2, 144, LANES), I16),
            pltpu.VMEM((2, 3, 2, 2, 144, LANES), I16),
            pltpu.VMEM((2, 4, LANES, LANES), F32),
            pltpu.VMEM((2, 4, 2, 80, LANES), I16),
            pltpu.VMEM((2, 8, 80, LANES), I16),
            pltpu.VMEM((2, 2, 64, LANES), F32),
            pltpu.VMEM((96, 96), BF16),
            dma((6,)),
            dma,
            dma,
            dma((2,)),
            dma((2,)),
            dma((2, 3, 2)),
            dma((2, 3, 2)),
            dma((2,)),
            dma((2,)),
        ],
        compiler_params=pltpu.CompilerParams(
            collective_id=0, has_side_effects=True, vmem_limit_bytes=60 << 20
        ),
        name="forces",
    )(
        slab_map,
        slab_map.reshape(8, LANES),
        tile_list.T,
        press,
        modes,
    )
    return (
        out.reshape(64, 2, 2, LANES).transpose(0, 2, 1, 3).reshape(64, 2, 2 * LANES)
    )


def solution(mesh):
    return jax.shard_map(
        on_device,
        mesh=mesh,
        in_specs=(P(("mode", "dof"), None), P(("mode", "dof"), None, "resp"), P(), P()),
        out_specs=P(("mode", "dof"), None, "resp"),
        check_vma=False,
    )
```

```python
import functools

import jax
import jax.numpy as jnp
from jax import lax
from jax.experimental import pallas as pl
from jax.experimental.pallas import tpu as pltpu
from jax.sharding import PartitionSpec as P

F32 = jnp.float32
BF16 = jnp.bfloat16
I16 = jnp.int16
LANES = 128
BROWS = 24
GROUP = 32
CHIPS = 16
TOP = 32760.0
STEP = 64.0


def encode(v):
    r = v.shape[0]
    v3 = v.reshape(r // 16, 16, LANES)
    top = jnp.maximum(jnp.max(jnp.abs(v3), axis=0), 2.0**-110)
    e = jnp.ceil(jnp.log2(top) * STEP)
    inv = jnp.exp2(e * (-1.0 / STEP)) * TOP
    code = jnp.round(v3 * inv[None]).astype(jnp.int32).reshape(r, LANES)
    return jnp.concatenate([code, e.astype(jnp.int32)], axis=0).astype(I16)


def decode(q):
    r = q.shape[0] - 16
    w = q.astype(jnp.int32).astype(F32)
    scale = jnp.exp2(w[r:] * (1.0 / STEP)) * (1.0 / TOP)
    return (w[:r].reshape(r // 16, 16, LANES) * scale[None]).reshape(r, LANES)


def kernel(
    slab_hbm,
    slabv_hbm,
    tiles_hbm,
    press_hbm,
    modes_hbm,
    out,
    slab,
    slabv,
    found,
    table,
    tiles,
    press,
    modes,
    bal,
    sendb,
    recv0,
    recv1,
    bt,
    xs,
    xr,
    acc,
    ys,
    yr,
    own,
    pick,
    load_sem,
    m_send,
    m_recv,
    a_send,
    a_recv,
    x_send,
    x_recv,
    y_send,
    y_recv,
):
    mode = lax.axis_index("mode")
    resp = lax.axis_index("resp")
    core = lax.axis_index("dof")
    me = mode * 2 + core
    x = lax.rem(mode, 4)
    yh = mode // 4
    barrier = pltpu.get_barrier_semaphore()

    def greet(k, carry):
        d = lax.rem(me + k, GROUP)
        pl.semaphore_signal(
            barrier, inc=1, device_id={"mode": d // 2, "dof": lax.rem(d, 2)}
        )
        return carry

    load_v = pltpu.make_async_copy(slabv_hbm, slabv, load_sem.at[4])
    load_v.start()
    load_s = pltpu.make_async_copy(slab_hbm, slab, load_sem.at[2])
    load_s.start()
    load_p = pltpu.make_async_copy(press_hbm, press, load_sem.at[0])
    load_p.start()
    load_m = pltpu.make_async_copy(modes_hbm, modes.at[core], load_sem.at[1])
    load_m.start()
    load_t = pltpu.make_async_copy(tiles_hbm, tiles, load_sem.at[3])
    load_t.start()
    lax.fori_loop(1, GROUP, greet, 0)

    load_v.wait()
    ids = slabv[...]
    local = jnp.where(ids // GROUP == me, lax.rem(ids, GROUP), 0)
    for shift in (1, 2, 4, 8, 16):
        local = local + pltpu.roll(local, LANES - shift, 1)
    found[...] = lax.rem(local, GROUP)
    to_smem = pltpu.make_async_copy(found, table, load_sem.at[5])
    to_smem.start()

    row = lax.broadcasted_iota(jnp.int32, (96, 96), 0)
    col = lax.broadcasted_iota(jnp.int32, (96, 96), 1)
    hit = jnp.zeros((96, 96), F32)
    for q in range(4):
        i = row - q * BROWS
        hit = hit + jnp.where((i >= 0) & (i < BROWS) & (col == 4 * i + q), 1.0, 0.0)
    pick[...] = hit.astype(BF16)

    def a_copy(h, d):
        return pltpu.make_async_remote_copy(
            src_ref=sendb.at[h, d],
            dst_ref=(recv0, recv1)[h].at[lax.rem(me - d + GROUP, GROUP)],
            send_sem=a_send.at[h],
            recv_sem=a_recv.at[h],
            device_id={"mode": d // 2, "dof": lax.rem(d, 2)},
        )

    def a_wait(sem):
        part = recv0.at[pl.ds(1, GROUP - 1)]
        pltpu.make_async_copy(part, part, sem).wait()

    load_s.wait()
    load_p.wait()
    to_smem.wait()
    pl.semaphore_wait(barrier, GROUP - 1)
    swap = pltpu.make_async_remote_copy(
        src_ref=modes_hbm,
        dst_ref=modes.at[core],
        send_sem=m_send,
        recv_sem=m_recv,
        device_id={"dof": 1 - core},
    )
    swap.start()

    def pack(m):
        parts = []
        for g in range(2):
            d = 2 * m + g
            block = press[table[d // 4, GROUP * lax.rem(d, 4)]]
            parts.append(jnp.dot(pick[...], block, preferred_element_type=F32))
        for h in range(2):
            for p in range(2):
                q = (h * 2 + p) * BROWS
                sendb[h, 2 * m + p] = jnp.concatenate(
                    [part[q : q + BROWS] for part in parts], axis=0
                ).astype(BF16)

    def chip(k):
        r = lax.rem(k, 3)
        step = jnp.where(r == 0, 2, jnp.where(r == 1, 1, 3))
        far = k < 12
        dy = jnp.where(far, step, 0)
        dx = jnp.where(far, lax.rem(core * 2 + k // 3, 4), step)
        return lax.rem(yh + dy, 4) * 4 + lax.rem(x + dx, 4)

    def pack_and_send(k, carry):
        m = chip(k)
        pack(m)
        for p in range(2):
            a_copy(0, 2 * m + p).start()
        return carry

    lax.fori_loop(0, CHIPS - 1, pack_and_send, 0, unroll=3)
    pack(mode)
    mate = mode * 2 + 1 - core
    recv0[0] = sendb[0, me]
    recv1[0] = sendb[1, me]
    a_copy(0, mate).start()

    def send(k, carry):
        for p in range(2):
            a_copy(1, 2 * chip(k) + p).start()
        return carry

    lax.fori_loop(0, CHIPS - 1, send, 0)
    a_copy(1, mate).start()
    load_m.wait()
    swap.wait()

    def across(t):
        return jnp.where(t == 0, 1, jnp.where(t == 1, 3, jnp.where(t == 2, 2, 0)))

    def x_copy(h, t, u):
        return pltpu.make_async_remote_copy(
            src_ref=xs.at[h, t, u],
            dst_ref=xr.at[h, t, u],
            send_sem=x_send.at[h, t, u],
            recv_sem=x_recv.at[h, t, u],
            device_id={"mode": yh * 4 + lax.rem(x + across(t), 4)},
        )

    def y_wait(sem):
        part = yr.at[0, pl.ds(1, 7)]
        pltpu.make_async_copy(part, part, sem).wait()

    def first_stage(h):
        a_wait(a_recv.at[h])

        def align(recv, i, carry):
            for g in range(2):
                parts = []
                for w in range(2):
                    q = slab[(2 * mode + g) * GROUP + 2 * i + w] // GROUP
                    slot = lax.rem(q - me + GROUP, GROUP)
                    both = recv[slot].astype(F32)
                    parts.append(both[g * BROWS : (g + 1) * BROWS])
                bal[g, i] = jnp.concatenate(parts, axis=0).astype(BF16)
            return carry

        for way, recv in enumerate((recv0, recv1)):

            @pl.when(h == way)
            def _():
                lax.fori_loop(0, GROUP // 2, functools.partial(align, recv), 0)

        bt[...] = bal[...].reshape(GROUP * 2 * BROWS, LANES).T

        def block(n, carry):
            u = n // 4
            t = lax.rem(n, 4)
            xt = lax.rem(x + across(t), 4)
            part = jnp.zeros((LANES, 2 * LANES), F32)
            for g in range(2):
                both = jnp.concatenate(
                    [
                        modes[g, :, pl.ds(((2 * u + w) * 4 + xt) * LANES, LANES)]
                        for w in range(2)
                    ],
                    axis=1,
                )
                depth = GROUP * BROWS
                part = part + jnp.dot(
                    bt[:, g * depth : (g + 1) * depth],
                    both,
                    preferred_element_type=F32,
                )
            halves = [part[:, w * LANES : (w + 1) * LANES] for w in range(2)]

            @pl.when(t == 3)
            def _():
                for w in range(2):
                    acc[h, 2 * u + w] = halves[w]

            @pl.when(t < 3)
            def _():
                for w in range(2):
                    xs[h, t, u, w] = encode(halves[w])
                x_copy(h, t, u).start()

            return carry

        lax.fori_loop(0, 8, block, 0)

    def second_stage(h, u):
        for t in range(3):
            x_copy(h, t, u).wait_recv()

        def block(v, carry):
            yt = 2 * u + v
            j = lax.rem(yt - yh + 4, 4)
            total = acc[h, yt]
            for t in range(3):
                total = total + decode(xr[h, t, u, v])
            turned = total.T

            @pl.when(j == 0)
            def _():
                own[h] = turned.reshape(2, 64, LANES)

            for w in range(2):
                ys[h, j, w] = encode(turned[64 * w : 64 * w + 64])

            def send(w, carry):
                to = lax.rem(core + w, 2)
                pltpu.make_async_remote_copy(
                    src_ref=ys.at[h, j, to],
                    dst_ref=yr.at[h, 2 * j + w],
                    send_sem=y_send.at[h],
                    recv_sem=y_recv.at[h],
                    device_id={"mode": yt * 4 + x, "dof": to},
                ).start()
                return carry

            lax.fori_loop(jnp.where(j == 0, 1, 0), 2, send, 0)
            return carry

        lax.fori_loop(0, 2, block, 0, unroll=True)

    def third_stage(h):
        mine = tiles[0:1, :] == mode
        lane = lax.broadcasted_iota(jnp.int32, (64, LANES), 1)
        keep = []
        for b in range(2):
            match = mine & (tiles[1:2, :] == resp * 4 + 2 * h + b)
            keep.append(jnp.max(jnp.where(match, 1.0, 0.0), axis=1, keepdims=True))
        mask = jnp.where(lane < 64, keep[0], keep[1])
        y_wait(y_recv.at[h])
        same = own[h, core]
        other = decode(yr[h, 1])
        for k in range(1, 4):
            same = same + decode(yr[h, 2 * k])
            other = other + decode(yr[h, 2 * k + 1])
        same = same * mask
        other = other * mask
        out[pl.ds(2 * h, 64, stride=4), :] = jnp.where(core == 0, same, other)
        out[pl.ds(2 * h + 1, 64, stride=4), :] = jnp.where(core == 0, other, same)

    def first(h, carry):
        first_stage(h)
        return carry

    def second(n, carry):
        second_stage(n // 2, lax.rem(n, 2))
        return carry

    def third(h, carry):
        third_stage(h)
        return carry

    lax.fori_loop(0, 2, first, 0)
    lax.fori_loop(0, 4, second, 0)
    load_t.wait()
    lax.fori_loop(0, 2, third, 0)

    a_wait(a_send.at[0])
    a_wait(a_send.at[1])
    for h in range(2):
        for t in range(3):
            for u in range(2):
                x_copy(h, t, u).wait_send()
        y_wait(y_send.at[h])


def on_device(modes, pressure, tile_list, slab_map):
    rows = pressure.shape[0]
    blocks = rows // BROWS
    press = (
        pressure.reshape(rows, 2, 2, LANES)
        .transpose(0, 2, 1, 3)
        .reshape(blocks, 4 * BROWS, LANES)
    )
    dma = pltpu.SemaphoreType.DMA
    wide = modes.shape[1]
    out = pl.pallas_call(
        kernel,
        out_shape=jax.ShapeDtypeStruct((256, LANES), F32),
        in_specs=[
            pl.BlockSpec(memory_space=pltpu.HBM),
            pl.BlockSpec(memory_space=pltpu.HBM),
            pl.BlockSpec(memory_space=pltpu.HBM),
            pl.BlockSpec(memory_space=pltpu.HBM),
            pl.BlockSpec(memory_space=pltpu.HBM),
        ],
        out_specs=pl.BlockSpec(memory_space=pltpu.VMEM),
        scratch_shapes=[
            pltpu.SMEM(slab_map.shape, jnp.int32),
            pltpu.VMEM((8, LANES), jnp.int32),
            pltpu.VMEM((8, LANES), jnp.int32),
            pltpu.SMEM((8, LANES), jnp.int32),
            pltpu.VMEM(tile_list.shape[::-1], jnp.int32),
            pltpu.VMEM((blocks, 4 * BROWS, LANES), BF16),
            pltpu.VMEM((2, rows, wide), BF16),
            pltpu.VMEM((2, blocks // 2, 2 * BROWS, LANES), BF16),
            pltpu.VMEM((2, GROUP, 2 * BROWS, LANES), BF16),
            pltpu.VMEM((GROUP, 2 * BROWS, LANES), BF16),
            pltpu.VMEM((GROUP, 2 * BROWS, LANES), BF16),
            pltpu.VMEM((LANES, GROUP * 2 * BROWS), BF16),
            pltpu.VMEM((2, 3, 2, 2, 144, LANES), I16),
            pltpu.VMEM((2, 3, 2, 2, 144, LANES), I16),
            pltpu.VMEM((2, 4, LANES, LANES), F32),
            pltpu.VMEM((2, 4, 2, 80, LANES), I16),
            pltpu.VMEM((2, 8, 80, LANES), I16),
            pltpu.VMEM((2, 2, 64, LANES), F32),
            pltpu.VMEM((96, 96), BF16),
            dma((6,)),
            dma,
            dma,
            dma((2,)),
            dma((2,)),
            dma((2, 3, 2)),
            dma((2, 3, 2)),
            dma((2,)),
            dma((2,)),
        ],
        compiler_params=pltpu.CompilerParams(
            collective_id=0, has_side_effects=True, vmem_limit_bytes=60 << 20
        ),
        name="forces",
    )(
        slab_map,
        slab_map.reshape(8, LANES),
        tile_list.T,
        press,
        modes,
    )
    return (
        out.reshape(64, 2, 2, LANES).transpose(0, 2, 1, 3).reshape(64, 2, 2 * LANES)
    )


def solution(mesh):
    return jax.shard_map(
        on_device,
        mesh=mesh,
        in_specs=(P(("mode", "dof"), None), P(("mode", "dof"), None, "resp"), P(), P()),
        out_specs=P(("mode", "dof"), None, "resp"),
        check_vma=False,
    )
```
